32 devices in a mesh: rows: 8 (over z, x), cols: 4 (over y, core).
Axes of the slice: x: 2, y: 2, z: 4, core: 2. Of those that a mesh axis runs over, the one named last changes fastest.
Arguments:
- front_rows: bfloat16 [8, 1024, 4096], P(None, 'rows', 'cols'), may hold values from -0.1875 to 0.1875
- heights: int32 [8, 8], P('rows'), may hold values from 1 to 128
- child_rows: bfloat16 [8192, 4096], P('rows', 'cols'), may hold values from -0.1875 to 0.1875
- child_dest: int32 [8192, 1], P('rows'), may hold values from 0 to 7; in each aligned block of 1024 rows (0 to 1023, 1024 to 2047, ...) at most 256 rows name the same one
- child_slot: int32 [8192], P('rows'), may hold values from 0 to 127
- parent_ids: int32 [128], P('rows'), may hold values from 0 to 7
Outputs:
- r_rows: float32 [8, 128, 4096], P(None, None, ('cols', 'rows'))
The draws below stay inside these ranges and needn't reach their ends.
Inputs may be any that keep to these rules, and one draw needn't show every extreme that they name: `child_dest`: in the rows of one device, at most 256 child rows name one index of rows.
All inputs are finite; a program needn't handle non-finite values.
Results may differ from the reference program's by a relative error of at most 0.002.
Values may be sent and summed in bfloat16 or wider, within the bound.
A program may use at most 64 MiB of HBM per device.

```python
import math
import jax
import jax.numpy as jnp
import numpy as np
from jax import lax

W = 4096
NB = 128
F = 8
HC = 128
CR = 1024
KB = 64
CAP = 256
KIDS = 128
N_ROWS = 8


def draw_heights(key, part):
    key_shift, key_spot = jax.random.split(jax.random.fold_in(key, 17), 2)
    halving = jax.random.randint(key_shift, (N_ROWS * F,), 0, 4)
    values = jnp.maximum(1, HC // jnp.power(2, halving))
    spot = jax.random.randint(key_spot, (), 0, N_ROWS * F)
    values = jnp.where(jnp.arange(N_ROWS * F) == spot, HC, values)
    return values.reshape(N_ROWS, F).astype(jnp.int32)


def with_ends(array, stream_key, least, high):
    longest = array.shape.index(max(array.shape))
    spots = []
    for shift in (0, 1):
        where = [jax.random.randint(jax.random.fold_in(stream_key, axis), (), 0, length) for axis, length in enumerate(array.shape)]
        where[longest] = (where[longest] + shift) % array.shape[longest]
        spots.append(tuple(where))
    return array.at[spots[0]].set(least).at[spots[1]].set(high)


def levels(key, extent, cuts, least, high):
    factor_of, own = 1.0, jax.random.fold_in(key, 6)
    for position, blocks in cuts:
        steps = jnp.exp(jax.random.uniform(jax.random.fold_in(own, position), (blocks,), jnp.float32, least / len(cuts), high / len(cuts)))
        factor_of = factor_of * jnp.repeat(steps, extent[position] // blocks).reshape([-1 if axis == position else 1 for axis in range(len(extent))])
    return factor_of


def deal_out(key, own, number, rows, count, top, limit, skew):
    sequence = jax.random.permutation(key, count)
    crowded, common = shares(count, rows * top, limit, skew, True), shares(count, rows * top, limit, skew, False)
    places = jnp.arange(count)

    def named(sizes, offset_by):
        used = int((sizes > 0).sum())
        fixed = max(1, used // 4)
        passed = fixed + (places - fixed + offset_by * (used - fixed)) % max(1, count - fixed)
        return jnp.zeros((count,), jnp.int32).at[sequence[jnp.where(places < fixed, places, passed)]].set(jnp.asarray(sizes, jnp.int32))

    sizes = jnp.where(number % 4 == 0, named(crowded, number // 4), named(common, number - number // 4 - 1))
    mixed = jax.random.permutation(jax.random.fold_in(own, 3), count)
    giver, taker = mixed[0:count // 2 * 2:2], mixed[1:count // 2 * 2:2]
    margin = jnp.minimum(sizes[giver] - 1, limit - sizes[taker]) // 2
    margin = jnp.where((giver == sequence[0]) | (taker == sequence[0]) | (sizes[taker] == 0), 0, jnp.maximum(margin, 0))
    passed = jax.random.randint(jax.random.fold_in(own, 4), (count // 2,), 0, 1 << 20) % (margin + 1)
    sizes = sizes.at[giver].add(-passed).at[taker].add(passed)
    items = jnp.searchsorted(jnp.cumsum(sizes), jnp.arange(rows * top), side="right").astype(jnp.int32)
    listing = items.reshape(top, rows).T
    listing = listing[jax.random.permutation(jax.random.fold_in(own, 1), rows)]
    offset_by = jax.random.randint(jax.random.fold_in(own, 2), (rows, 1), 0, top)
    return jnp.take_along_axis(listing, (jnp.arange(top)[None, :] + offset_by) % top, axis=1)


def shares(number_of, total, reach, skew, full):
    weights = [(1 << 20) // math.isqrt(rank ** skew) + 1 for rank in range(1, number_of + 1)]
    largest = reach if full else min(reach, max(-(-total // number_of), total * weights[0] // sum(weights)))
    least = 1 if total - largest >= number_of - 1 else 0
    counts, spare = [largest] + [least] * (number_of - 1), total - largest - least * (number_of - 1)
    while spare > 0:
        free = [i for i in range(1, number_of) if counts[i] < largest] or [i for i in range(1, number_of) if counts[i] < reach]
        whole, budget = sum([weights[i] for i in free]), spare
        for i in free:
            more = min(reach - counts[i], max(1, budget * weights[i] // whole), spare)
            counts[i] = counts[i] + more
            spare = spare - more
    return np.array(counts)


def gaussian(stream_key, extent, width, limit, shards=(), held_as=jnp.bfloat16):
    result = jax.random.normal(stream_key, extent, jnp.float32) * width
    if len(shards) > 0:
        result = levels(stream_key, extent, shards, -0.22, 0.18) * result
    return jnp.clip(result, min=-limit, max=limit).astype(held_as)


def setup_inputs(seed: int = 0) -> dict:
    splits = jax.random.split(jax.random.key(seed), 7)
    front_rows = gaussian(splits[0], (F, N_ROWS * HC, W), ((N_ROWS * HC) ** -0.5), 0.1875, ((1, 8), (2, 4)))
    heights = draw_heights(jax.random.fold_in(splits[6], 71), 0)
    child_rows = gaussian(splits[2], (N_ROWS * CR, W), ((N_ROWS * HC) ** -0.5), 0.1875, ((0, 8), (1, 4)))
    child_dest_keys = jax.random.split(jax.random.fold_in(splits[3], 1), (N_ROWS * CR) // CR)
    child_dest_turns = jax.random.permutation(jax.random.fold_in(splits[3], 3), (N_ROWS * CR) // CR)
    child_dest = jax.vmap(lambda own, number: deal_out(jax.random.fold_in(splits[3], 2), own, number, CR, N_ROWS, 1, CAP, 2))(child_dest_keys, child_dest_turns).reshape((N_ROWS * CR, 1))
    child_slot = with_ends(jax.random.randint(splits[4], (N_ROWS * CR,), 0, HC), jax.random.fold_in(splits[4], 1), 0, HC - 1).astype(jnp.int32)
    parent_ids = with_ends(jax.random.randint(splits[5], (KIDS,), 0, F), jax.random.fold_in(splits[5], 1), 0, F - 1).astype(jnp.int32)
    return {"front_rows": front_rows, "heights": heights, "child_rows": child_rows, "child_dest": child_dest, "child_slot": child_slot, "parent_ids": parent_ids}


def reference(front_rows, heights, child_rows, child_dest, child_slot, parent_ids):
    own_rows = front_rows.reshape(F, N_ROWS, HC, W)
    live_mask = jnp.arange(HC, dtype=jnp.int32)[None, None, :] < jnp.transpose(heights)[:, :, None]
    child_front = jnp.repeat(parent_ids, KB)
    target = child_dest[:, 0] * HC + child_slot
    child_lead = child_rows[:, :NB].astype(jnp.float32)

    def one_front(front):
        base = jnp.where(live_mask[front][:, :, None], own_rows[front], jnp.zeros((), jnp.bfloat16))
        base = base.reshape(N_ROWS * HC, W)
        belongs = child_front == front
        weight = belongs.astype(jnp.float32)
        added = jnp.zeros((N_ROWS * HC, NB), jnp.float32).at[target].add(child_lead * weight[:, None])
        panel = (base[:, :NB].astype(jnp.float32) + added).astype(jnp.bfloat16)
        picked = jnp.where(belongs[:, None], panel[target], jnp.zeros((), jnp.bfloat16))
        cross = jnp.dot(panel.T.astype(jnp.float32), base.astype(jnp.float32), preferred_element_type=jnp.float32)
        cross = cross + jnp.dot(picked.T.astype(jnp.float32), child_rows.astype(jnp.float32), preferred_element_type=jnp.float32)
        gram = jnp.dot(panel.T.astype(jnp.float32), panel.astype(jnp.float32), preferred_element_type=jnp.float32)
        lower = jnp.linalg.cholesky(gram)
        return jax.scipy.linalg.solve_triangular(lower, cross, lower=True)
    return lax.map(one_front, jnp.arange(F, dtype=jnp.int32))
```

```python
import jax
import jax.numpy as jnp
from jax import lax
from jax.experimental import pallas as pl
from jax.experimental.pallas import tpu as pltpu
from jax.sharding import PartitionSpec as P

NB = 128


def lane(x, index):
    return jnp.take_along_axis(x, jnp.full(x.shape, index, jnp.int32), axis=1)


def inverse_factor(a, b):
    step = 8
    ids = lax.broadcasted_iota(jnp.int32, b.shape[1:], 1)

    def unit(i, carry):
        b[i] = (ids == i).astype(jnp.float32)
        return carry

    lax.fori_loop(0, NB, unit, 0)

    def block(at, carry):
        base = at * step
        rows = [a[base + k] for k in range(step)]
        right = [b[base + k] for k in range(step)]
        for k in range(step):
            pivot = lane(rows[k], base + k)
            inverse = 1.0 / pivot
            root = lax.rsqrt(pivot)
            for m in range(k + 1, step):
                scale = lane(rows[k], base + m) * inverse
                rows[m] = rows[m] - scale * rows[k]
                right[m] = right[m] - scale * right[k]
            rows[k] = rows[k] * root
            right[k] = right[k] * root
            b[base + k] = right[k]

        def below(quad, inner):
            for u in range(4):
                i = quad * 4 + u
                left_row, right_row = a[i], b[i]
                for k in range(step):
                    scale = lane(rows[k], i)
                    left_row = left_row - scale * rows[k]
                    right_row = right_row - scale * right[k]
                a[i] = left_row
                b[i] = right_row
            return inner

        lax.fori_loop((base + step) // 4, NB // 4, below, 0)
        return carry

    lax.fori_loop(0, NB // step, block, 0)


def factor_kernel(gram_ref, out_ref, a, b):
    fronts = gram_ref.shape[0]
    for f in range(fronts):
        a[:, f, :] = gram_ref[f]
    inverse_factor(a, b)
    for f in range(fronts):
        out_ref[f] = b[:, f, :]


def factor(gram):
    fronts = gram.shape[0]
    return pl.pallas_call(
        factor_kernel,
        out_shape=jax.ShapeDtypeStruct(gram.shape, jnp.float32),
        in_specs=[pl.BlockSpec(memory_space=pltpu.VMEM)],
        out_specs=pl.BlockSpec(memory_space=pltpu.VMEM),
        scratch_shapes=[pltpu.VMEM((NB, fronts, NB), jnp.float32)] * 2,
        compiler_params=pltpu.CompilerParams(vmem_limit_bytes=8 << 20),
        cost_estimate=pl.CostEstimate(flops=40_000_000_000, bytes_accessed=1 << 20, transcendentals=0),
    )(gram)


def on_device(front_rows, heights, child_rows, child_dest, child_slot, parent_ids):
    fronts, height_cap, width = front_rows.shape
    peers = lax.axis_size("rows")
    count = child_rows.shape[0]
    capacity = max(2, 2 * count // peers)
    slots = peers * capacity
    local_rows = fronts * height_cap
    destination = child_dest[:, 0]
    child_front = jnp.repeat(parent_ids, count // parent_ids.shape[0])
    hits = (destination[:, None] == jnp.arange(peers, dtype=jnp.int32)[None, :]).astype(jnp.bfloat16)
    earlier = (jnp.arange(count)[:, None] > jnp.arange(count)[None, :]).astype(jnp.bfloat16)
    before = jnp.dot(earlier, hits, preferred_element_type=jnp.float32)
    position = jnp.sum(before * hits.astype(jnp.float32), axis=1).astype(jnp.int32)
    send_index = destination * capacity + position
    packing = (jnp.arange(slots, dtype=jnp.int32)[:, None] == send_index[None, :]).astype(jnp.bfloat16)
    send_lead = jnp.dot(packing, child_rows[:, :NB], preferred_element_type=jnp.float32).astype(jnp.bfloat16)
    tags = jnp.stack([child_front, child_slot], axis=0).astype(jnp.bfloat16)
    send_tags = lax.dot_general(
        tags, packing, (((1,), (1,)), ((), ())), preferred_element_type=jnp.float32
    ).astype(jnp.bfloat16)
    tag_rows = -(-2 * capacity // NB)
    send_tags = jnp.transpose(send_tags.reshape(2, peers, capacity), (1, 0, 2)).reshape(peers, 2 * capacity)
    send_tags = jnp.pad(send_tags, ((0, 0), (0, tag_rows * NB - 2 * capacity))).reshape(peers, tag_rows, NB)
    sent = jnp.concatenate([send_lead.reshape(peers, capacity, NB), send_tags], axis=1)
    got = lax.all_to_all(sent, "rows", split_axis=0, concat_axis=0, tiled=True)
    got_lead = got[:, :capacity].reshape(slots, NB)
    got_tags = got[:, capacity:].reshape(peers, tag_rows * NB)[:, : 2 * capacity].astype(jnp.int32)
    got_tags = got_tags.reshape(peers, 2, capacity)
    target = (got_tags[:, 0] * height_cap + got_tags[:, 1]).reshape(slots)
    placing = (jnp.arange(local_rows, dtype=jnp.int32)[:, None] == target[None, :]).astype(jnp.bfloat16)
    added = jnp.dot(placing, got_lead, preferred_element_type=jnp.float32)
    live_mask = jnp.arange(height_cap, dtype=jnp.int32)[None, :] < heights[0][:, None]
    own = jnp.where(live_mask[:, :, None], front_rows, jnp.zeros_like(front_rows))
    panel_own = (own[:, :, :NB].reshape(local_rows, NB).astype(jnp.float32) + added).astype(jnp.bfloat16)
    panel_own = lax.psum(
        jnp.where(lax.axis_index("cols") == 0, panel_own, jnp.zeros_like(panel_own)), "cols"
    )
    panel_all = lax.all_gather(panel_own, "rows", axis=0, tiled=True)
    by_front = panel_all.reshape(peers, fronts, height_cap, NB)
    gram = jnp.einsum("pfhk,pfhj->fkj", by_front, by_front, preferred_element_type=jnp.float32)
    key = destination * local_rows + child_front * height_cap + child_slot
    choosing = (key[:, None] == jnp.arange(peers * local_rows, dtype=jnp.int32)[None, :]).astype(jnp.bfloat16)
    selected = jnp.dot(choosing, panel_all, preferred_element_type=jnp.float32).astype(jnp.bfloat16)
    which = (jnp.arange(fronts, dtype=jnp.int32)[:, None] == child_front[None, :]).astype(jnp.bfloat16)
    picked = which[:, :, None] * selected[None, :, :]
    local = jnp.einsum("fsk,sc->fkc", picked, child_rows, preferred_element_type=jnp.float32)
    local = local + jnp.einsum(
        "fhk,fhc->fkc", panel_own.reshape(fronts, height_cap, NB), own, preferred_element_type=jnp.float32
    )
    columns = lax.psum_scatter(
        jnp.transpose(local.reshape(fronts, NB, peers, width // peers), (2, 0, 1, 3)),
        "rows",
        scatter_dimension=0,
        tiled=True,
    )[0]
    inverse = factor(gram)
    return jnp.einsum(
        "fij,fjc->fic", inverse, columns, precision=lax.Precision.HIGHEST, preferred_element_type=jnp.float32
    )


def solution(mesh):
    placed = (
        P(None, "rows", "cols"),
        P("rows", None),
        P("rows", "cols"),
        P("rows", None),
        P("rows"),
        P("rows"),
    )
    return jax.shard_map(
        on_device,
        mesh=mesh,
        in_specs=placed,
        out_specs=P(None, None, ("cols", "rows")),
        check_vma=False,
    )
```

```python
import functools
import math

import jax
import jax.numpy as jnp
from jax import lax
from jax.experimental import pallas as pl
from jax.experimental.pallas import tpu as pltpu
from jax.sharding import PartitionSpec as P

NB = 128
LARGEST = 0.1875
MESH = pl.DeviceIdType.MESH


def lane(x, index):
    return jnp.take_along_axis(x, jnp.full(x.shape, index, jnp.int32), axis=1, mode="promise_in_bounds")


def inverse_factor(a, b):
    step = 8
    ids = lax.broadcasted_iota(jnp.int32, b.shape[1:], 1)

    def unit(i, carry):
        b[i] = (ids == i).astype(jnp.float32)
        return carry

    lax.fori_loop(0, NB, unit, 0)

    def block(at, carry, end):
        base = at * step
        rows = [a[base + k] for k in range(step)]
        right = [b[base + k] for k in range(step)]
        for k in range(step):
            pivot = lane(rows[k], base + k)
            inverse = 1.0 / pivot
            root = lax.rsqrt(pivot)
            for m in range(k + 1, step):
                scale = lane(rows[k], base + m) * inverse
                rows[m] = rows[m] - scale * rows[k]
                right[m] = right[m] - scale * right[k]
            rows[k] = rows[k] * root
            right[k] = right[k] * root
            a[base + k] = rows[k]
            b[base + k] = right[k]

        def below(quad, inner):
            for u in range(4):
                i = quad * 4 + u
                left_row, right_row = a[i], b[i]
                for k in range(step):
                    scale = lane(rows[k], i)
                    left_row = left_row - scale * rows[k]
                    right_row = right_row - scale * right[k]
                a[i] = left_row
                b[i] = right_row
            return inner

        lax.fori_loop((base + step) // 4, end // 4, below, 0)
        return carry

    group = 32
    for start in range(0, NB, group):
        end = start + group
        lax.fori_loop(start // step, end // step, functools.partial(block, end=end), 0)
        if end < NB:
            for f in range(a.shape[1]):
                left, right = a[start:end, f, :], b[start:end, f, :]
                turned = left.T[end:]
                a[end:, f, :] -= jnp.dot(
                    turned, left, precision=lax.Precision.HIGHEST, preferred_element_type=jnp.float32
                )
                b[end:, f, :] -= jnp.dot(
                    turned, right, precision=lax.Precision.HIGHEST, preferred_element_type=jnp.float32
                )


def factor_kernel(gram_ref, out_ref, a, b):
    fronts = gram_ref.shape[0]
    for f in range(fronts):
        a[:, f, :] = gram_ref[f]
    inverse_factor(a, b)
    for f in range(fronts):
        out_ref[f] = b[:, f, :]


def factor(gram):
    fronts = gram.shape[0]
    return pl.pallas_call(
        factor_kernel,
        out_shape=jax.ShapeDtypeStruct(gram.shape, jnp.float32),
        in_specs=[pl.BlockSpec(memory_space=pltpu.VMEM)],
        out_specs=pl.BlockSpec(memory_space=pltpu.VMEM),
        scratch_shapes=[pltpu.VMEM((NB, fronts, NB), jnp.float32)] * 2,
        compiler_params=pltpu.CompilerParams(vmem_limit_bytes=8 << 20),
        cost_estimate=pl.CostEstimate(flops=40_000_000_000, bytes_accessed=1 << 20, transcendentals=0),
    )(gram)


def panel_kernel(
    peers, cols, lead_ref, target_ref, own_ref, out_ref,
    got_lead, got_target, total, panel,
    lead_send, lead_recv, target_send, target_recv, part_send, part_recv,
    row_send, row_recv, pair_send, pair_recv, core_send, core_recv, home,
):
    me, col = lax.axis_index("rows"), lax.axis_index("cols")
    pairs = cols // 2
    core, pair = lax.rem(col, 2), lax.div(col, 2)
    twin = pair * 2 + 1 - core
    rows = own_ref.shape[0]
    part = rows // cols
    chunks = lead_ref.shape[1] // NB

    def at(r, c):
        return {"rows": r, "cols": c}

    barrier = pltpu.get_barrier_semaphore()
    for k in range(1, peers):
        pl.semaphore_signal(barrier, inc=1, device_id=at(lax.rem(me + k, peers), col), device_id_type=MESH)
    for k in range(1, cols):
        pl.semaphore_signal(barrier, inc=1, device_id=at(me, lax.rem(col + k, cols)), device_id_type=MESH)
    pl.semaphore_wait(barrier, peers + cols - 2)

    def lead_copy(to, slot_from, slot):
        return (
            pltpu.make_async_remote_copy(
                src_ref=lead_ref.at[slot_from], dst_ref=got_lead.at[slot],
                send_sem=lead_send.at[slot_from], recv_sem=lead_recv.at[slot],
                device_id=at(to, 0), device_id_type=MESH,
            ),
            pltpu.make_async_remote_copy(
                src_ref=target_ref.at[slot_from], dst_ref=got_target.at[slot],
                send_sem=target_send.at[slot_from], recv_sem=target_recv.at[slot],
                device_id=at(to, 0), device_id_type=MESH,
            ),
        )

    def part_copy(index):
        where = pl.ds(pl.multiple_of(index * part, 16), part)
        return pltpu.make_async_remote_copy(
            src_ref=panel.at[where], dst_ref=panel.at[where],
            send_sem=part_send.at[index], recv_sem=part_recv.at[index],
            device_id=at(me, index), device_id_type=MESH,
        )

    def placed(target, lead):
        ids = lax.broadcasted_iota(jnp.int32, (rows, NB), 0).astype(jnp.float32)
        chosen = jnp.where(ids == target, 1.0, 0.0).astype(jnp.bfloat16)
        return jnp.dot(chosen, lead, preferred_element_type=jnp.float32)

    @pl.when(col == 0)
    def _():
        def send(k, carry):
            to = lax.rem(me + k, peers)
            for copy in lead_copy(to, to, me):
                copy.start()
            return carry

        lax.fori_loop(1, peers, send, 0)
        total[...] = own_ref[...].astype(jnp.float32)
        for u in range(chunks):
            total[...] += placed(target_ref[me, pl.ds(u, 1), :], lead_ref[me, pl.ds(u * NB, NB), :])

        def take(k, carry):
            source = lax.rem(me + peers - k, peers)
            for copy in lead_copy(source, source, source):
                copy.wait_recv()
            for u in range(chunks):
                total[...] += placed(got_target[source, pl.ds(u, 1), :], got_lead[source, pl.ds(u * NB, NB), :])
            return carry

        lax.fori_loop(1, peers, take, 0)
        panel[...] = total[...].astype(jnp.bfloat16)
        for index in range(1, cols):
            part_copy(index).start()

    @pl.when(col != 0)
    def _():
        part_copy(col).wait_recv()

    mine = pl.ds(pl.multiple_of(col * part, 16), part)

    def row_copy(k, source):
        return pltpu.make_async_remote_copy(
            src_ref=panel.at[mine], dst_ref=out_ref.at[source, mine],
            send_sem=row_send.at[k], recv_sem=row_recv.at[source],
            device_id=at(lax.rem(me + k, peers), col), device_id_type=MESH,
        )

    def pair_copy(source, k, owner):
        where = pl.ds(pl.multiple_of((owner * 2 + core) * part, 16), part)
        return pltpu.make_async_remote_copy(
            src_ref=out_ref.at[source, where], dst_ref=out_ref.at[source, where],
            send_sem=pair_send.at[source, k], recv_sem=pair_recv.at[source, owner],
            device_id=at(me, lax.rem(pair + k, pairs) * 2 + core), device_id_type=MESH,
        )

    def core_copy(source, owner, side):
        where = pl.ds(pl.multiple_of((owner * 2 + side) * part, 16), part)
        return pltpu.make_async_remote_copy(
            src_ref=out_ref.at[source, where], dst_ref=out_ref.at[source, where],
            send_sem=core_send.at[source, owner], recv_sem=core_recv.at[source, owner],
            device_id=at(me, twin), device_id_type=MESH,
        )

    def push(k, carry):
        row_copy(k, me).start()
        return carry

    lax.fori_loop(1, peers, push, 0)
    local = pltpu.make_async_copy(panel.at[mine], out_ref.at[me, mine], home)
    local.start()
    local.wait()

    def relay(source):
        for k in range(1, pairs):
            pair_copy(source, k, pair).start()
        core_copy(source, pair, core).start()

    def onward(source):
        for k in range(1, pairs):
            owner = lax.rem(pair + k, pairs)
            pair_copy(source, k, owner).wait_recv()
            core_copy(source, owner, core).start()

    relay(me)

    def step(k, carry):
        source = lax.rem(me + peers - k, peers)
        row_copy(k, source).wait_recv()
        relay(source)
        onward(lax.rem(source + 1, peers))
        return carry

    lax.fori_loop(1, peers, step, 0)
    onward(lax.rem(me + 1, peers))

    def finish(source, carry):
        for owner in range(pairs):
            core_copy(source, owner, 1 - core).wait_recv()
            core_copy(source, owner, core).wait_send()
        for k in range(1, pairs):
            pair_copy(source, k, pair).wait_send()
        return carry

    lax.fori_loop(0, peers, finish, 0)

    def sent(k, carry):
        row_copy(k, me).wait_send()
        return carry

    lax.fori_loop(1, peers, sent, 0)

    @pl.when(col == 0)
    def _():
        def leads(k, carry):
            to = lax.rem(me + k, peers)
            for copy in lead_copy(to, to, me):
                copy.wait_send()
            return carry

        lax.fori_loop(1, peers, leads, 0)
        for index in range(1, cols):
            part_copy(index).wait_send()


def gather_panel(leads, targets, own):
    peers, cols = lax.axis_size("rows"), lax.axis_size("cols")
    pairs = cols // 2
    vmem = pl.BlockSpec(memory_space=pltpu.VMEM)
    dma = pltpu.SemaphoreType.DMA
    return pl.pallas_call(
        functools.partial(panel_kernel, peers, cols),
        out_shape=jax.ShapeDtypeStruct((peers,) + own.shape, jnp.bfloat16),
        in_specs=[vmem] * 3,
        out_specs=pl.BlockSpec(memory_space=pl.ANY),
        scratch_shapes=[
            pltpu.VMEM(leads.shape, leads.dtype),
            pltpu.VMEM(targets.shape, targets.dtype),
            pltpu.VMEM(own.shape, jnp.float32),
            pltpu.VMEM(own.shape, jnp.bfloat16),
            dma((peers,)), dma((peers,)), dma((peers,)), dma((peers,)),
            dma((cols,)), dma((cols,)),
            dma((peers,)), dma((peers,)),
            dma((peers, pairs)), dma((peers, pairs)),
            dma((peers, pairs)), dma((peers, pairs)),
            dma,
        ],
        compiler_params=pltpu.CompilerParams(
            collective_id=0, has_side_effects=True, vmem_limit_bytes=40 << 20
        ),
        cost_estimate=pl.CostEstimate(flops=1 << 30, bytes_accessed=8 << 20, transcendentals=0),
    )(leads, targets, own)


def on_device(front_rows, heights, child_rows, child_dest, child_slot, parent_ids):
    fronts, height_cap, width = front_rows.shape
    peers = lax.axis_size("rows")
    count = child_rows.shape[0]
    capacity = -(-max(2, 2 * count // peers) // NB) * NB
    slots = peers * capacity
    local_rows = fronts * height_cap
    destination = child_dest[:, 0]
    child_front = jnp.repeat(parent_ids, count // parent_ids.shape[0])
    hits = (destination[:, None] == jnp.arange(peers, dtype=jnp.int32)[None, :]).astype(jnp.bfloat16)
    earlier = (jnp.arange(count)[:, None] > jnp.arange(count)[None, :]).astype(jnp.bfloat16)
    before = jnp.dot(earlier, hits, preferred_element_type=jnp.float32)
    position = jnp.sum(before * hits.astype(jnp.float32), axis=1).astype(jnp.int32)
    send_index = destination * capacity + position
    packing = (jnp.arange(slots, dtype=jnp.int32)[:, None] == send_index[None, :]).astype(jnp.bfloat16)
    send_lead = jnp.dot(packing, child_rows[:, :NB], preferred_element_type=jnp.float32).astype(jnp.bfloat16)
    tags = jnp.stack([child_front, child_slot], axis=0).astype(jnp.bfloat16)
    send_tags = lax.dot_general(
        tags, packing, (((1,), (1,)), ((), ())), preferred_element_type=jnp.float32
    )
    targets = (send_tags[0] * height_cap + send_tags[1]).reshape(peers, capacity // NB, NB)
    targets = jnp.pad(targets, ((0, 0), (0, -(capacity // NB) % 8), (0, 0)))
    live_mask = jnp.arange(height_cap, dtype=jnp.int32)[None, :] < heights[0][:, None]
    own = jnp.where(live_mask[:, :, None], front_rows, jnp.zeros_like(front_rows))
    gathered = gather_panel(
        send_lead.reshape(peers, capacity, NB), targets, own[:, :, :NB].reshape(local_rows, NB)
    )
    panel_own = lax.dynamic_index_in_dim(gathered, lax.axis_index("rows"), 0, keepdims=False)
    panel_all = gathered.reshape(peers * local_rows, NB)
    by_front = panel_all.reshape(peers, fronts, height_cap, NB)
    gram = jnp.einsum("pfhk,pfhj->fkj", by_front, by_front, preferred_element_type=jnp.float32)
    key = destination * local_rows + child_front * height_cap + child_slot
    choosing = (key[:, None] == jnp.arange(peers * local_rows, dtype=jnp.int32)[None, :]).astype(jnp.bfloat16)
    selected = jnp.dot(choosing, panel_all, preferred_element_type=jnp.float32).astype(jnp.bfloat16)
    which = (jnp.arange(fronts, dtype=jnp.int32)[:, None] == child_front[None, :]).astype(jnp.bfloat16)
    picked = which[:, :, None] * selected[None, :, :]
    local = jnp.einsum("fsk,sc->fkc", picked, child_rows, preferred_element_type=jnp.float32)
    local = local + jnp.einsum(
        "fhk,fhc->fkc", panel_own.reshape(fronts, height_cap, NB), own, preferred_element_type=jnp.float32
    )
    norm = jnp.sqrt(jnp.diagonal(gram, axis1=1, axis2=2))
    reach = LARGEST * math.sqrt(height_cap + count) * math.sqrt(2 * count // peers + 2)
    scale = norm * (reach / 60000.0)
    local = local * (1.0 / scale)[:, :, None]
    parts = jnp.transpose(local.reshape(fronts, NB, peers, width // peers), (2, 0, 1, 3)).astype(jnp.float16)
    parts = lax.all_to_all(parts, "rows", split_axis=0, concat_axis=0, tiled=True)
    columns = jnp.sum(parts.astype(jnp.float32), axis=0) * scale[:, :, None]
    inverse = factor(gram)
    return jnp.einsum(
        "fij,fjc->fic", inverse, columns, precision=lax.Precision.HIGHEST, preferred_element_type=jnp.float32
    )


def solution(mesh):
    placed = (
        P(None, "rows", "cols"),
        P("rows", None),
        P("rows", "cols"),
        P("rows", None),
        P("rows"),
        P("rows"),
    )
    return jax.shard_map(
        on_device,
        mesh=mesh,
        in_specs=placed,
        out_specs=P(None, None, ("cols", "rows")),
        check_vma=False,
    )
```

```python
import functools
import math

import jax
import jax.numpy as jnp
from jax import lax
from jax.experimental import pallas as pl
from jax.experimental.pallas import tpu as pltpu
from jax.sharding import PartitionSpec as P

NB = 128
LARGEST = 0.1875
MESH = pl.DeviceIdType.MESH


def lane(x, index):
    return jnp.take_along_axis(x, jnp.full(x.shape, index, jnp.int32), axis=1, mode="promise_in_bounds")


def inverse_factor(a, b):
    step = 8
    ids = lax.broadcasted_iota(jnp.int32, b.shape[1:], 1)

    def unit(i, carry):
        b[i] = (ids == i).astype(jnp.float32)
        return carry

    lax.fori_loop(0, NB, unit, 0)

    def block(at, carry, end):
        base = at * step
        rows = [a[base + k] for k in range(step)]
        right = [b[base + k] for k in range(step)]
        for k in range(step):
            pivot = lane(rows[k], base + k)
            inverse = 1.0 / pivot
            root = lax.rsqrt(pivot)
            for m in range(k + 1, step):
                scale = lane(rows[k], base + m) * inverse
                rows[m] = rows[m] - scale * rows[k]
                right[m] = right[m] - scale * right[k]
            rows[k] = rows[k] * root
            right[k] = right[k] * root
            a[base + k] = rows[k]
            b[base + k] = right[k]

        def below(quad, inner):
            for u in range(4):
                i = quad * 4 + u
                left_row, right_row = a[i], b[i]
                for k in range(step):
                    scale = lane(rows[k], i)
                    left_row = left_row - scale * rows[k]
                    right_row = right_row - scale * right[k]
                a[i] = left_row
                b[i] = right_row
            return inner

        lax.fori_loop((base + step) // 4, end // 4, below, 0)
        return carry

    group = 32
    for start in range(0, NB, group):
        end = start + group
        lax.fori_loop(start // step, end // step, functools.partial(block, end=end), 0)
        if end < NB:
            for f in range(a.shape[1]):
                left, right = a[start:end, f, :], b[start:end, f, :]
                turned = left.T[end:]
                a[end:, f, :] -= jnp.dot(
                    turned, left, precision=lax.Precision.HIGHEST, preferred_element_type=jnp.float32
                )
                b[end:, f, :] -= jnp.dot(
                    turned, right, precision=lax.Precision.HIGHEST, preferred_element_type=jnp.float32
                )


def factor_kernel(gram_ref, out_ref, a, b):
    fronts = gram_ref.shape[0]
    for f in range(fronts):
        a[:, f, :] = gram_ref[f]
    inverse_factor(a, b)
    for f in range(fronts):
        out_ref[f] = b[:, f, :]


def factor(gram):
    fronts = gram.shape[0]
    return pl.pallas_call(
        factor_kernel,
        out_shape=jax.ShapeDtypeStruct(gram.shape, jnp.float32),
        in_specs=[pl.BlockSpec(memory_space=pltpu.VMEM)],
        out_specs=pl.BlockSpec(memory_space=pltpu.VMEM),
        scratch_shapes=[pltpu.VMEM((NB, fronts, NB), jnp.float32)] * 2,
        compiler_params=pltpu.CompilerParams(vmem_limit_bytes=8 << 20),
        cost_estimate=pl.CostEstimate(flops=40_000_000_000, bytes_accessed=1 << 20, transcendentals=0),
    )(gram)


def panel_kernel(
    peers, cols, lead_ref, target_ref, own_ref, out_ref,
    got_lead, got_target, total, panel,
    lead_send, lead_recv, target_send, target_recv, part_send, part_recv,
    row_send, row_recv, pair_send, pair_recv, core_send, core_recv, home,
):
    me, col = lax.axis_index("rows"), lax.axis_index("cols")
    pairs = cols // 2
    core, pair = lax.rem(col, 2), lax.div(col, 2)
    twin = pair * 2 + 1 - core
    rows = own_ref.shape[0]
    part = rows // cols
    chunks = lead_ref.shape[1] // NB

    def at(r, c):
        return {"rows": r, "cols": c}

    barrier = pltpu.get_barrier_semaphore()
    for k in range(1, peers):
        pl.semaphore_signal(barrier, inc=1, device_id=at(lax.rem(me + k, peers), col), device_id_type=MESH)
    for k in range(1, cols):
        pl.semaphore_signal(barrier, inc=1, device_id=at(me, lax.rem(col + k, cols)), device_id_type=MESH)
    pl.semaphore_wait(barrier, peers + cols - 2)

    def lead_copy(to, slot_from, slot):
        return (
            pltpu.make_async_remote_copy(
                src_ref=lead_ref.at[slot_from], dst_ref=got_lead.at[slot],
                send_sem=lead_send.at[slot_from], recv_sem=lead_recv.at[slot],
                device_id=at(to, 0), device_id_type=MESH,
            ),
            pltpu.make_async_remote_copy(
                src_ref=target_ref.at[slot_from], dst_ref=got_target.at[slot],
                send_sem=target_send.at[slot_from], recv_sem=target_recv.at[slot],
                device_id=at(to, 0), device_id_type=MESH,
            ),
        )

    def part_copy(index):
        where = pl.ds(pl.multiple_of(index * part, 16), part)
        return pltpu.make_async_remote_copy(
            src_ref=panel.at[where], dst_ref=panel.at[where],
            send_sem=part_send.at[index], recv_sem=part_recv.at[index],
            device_id=at(me, index), device_id_type=MESH,
        )

    def placed(target, lead):
        ids = lax.broadcasted_iota(jnp.int32, (rows, target.shape[1]), 0).astype(jnp.float32)
        chosen = jnp.where(ids == target, 1.0, 0.0).astype(jnp.bfloat16)
        return jnp.dot(chosen, lead, preferred_element_type=jnp.float32)

    def spread(ref, source):
        return jnp.concatenate([ref[source, pl.ds(u, 1), :] for u in range(chunks)], axis=1)

    @pl.when(col == 0)
    def _():
        def send(k, carry):
            to = lax.rem(me + k, peers)
            for copy in lead_copy(to, to, me):
                copy.start()
            return carry

        lax.fori_loop(1, peers, send, 0)
        total[...] = own_ref[...].astype(jnp.float32)
        total[...] += placed(spread(target_ref, me), lead_ref[me])

        def take(k, carry):
            source = lax.rem(me + peers - k, peers)
            for copy in lead_copy(source, source, source):
                copy.wait_recv()
            total[...] += placed(spread(got_target, source), got_lead[source])
            return carry

        lax.fori_loop(1, peers, take, 0)
        panel[...] = total[...].astype(jnp.bfloat16)
        for index in range(cols - 1, 0, -1):
            part_copy(index).start()

    @pl.when(col != 0)
    def _():
        part_copy(col).wait_recv()

    mine = pl.ds(pl.multiple_of(col * part, 16), part)

    def row_copy(k, source):
        return pltpu.make_async_remote_copy(
            src_ref=panel.at[mine], dst_ref=out_ref.at[source, mine],
            send_sem=row_send.at[k], recv_sem=row_recv.at[source],
            device_id=at(lax.rem(me + k, peers), col), device_id_type=MESH,
        )

    def pair_copy(source, k, owner):
        where = pl.ds(pl.multiple_of((owner * 2 + core) * part, 16), part)
        return pltpu.make_async_remote_copy(
            src_ref=out_ref.at[source, where], dst_ref=out_ref.at[source, where],
            send_sem=pair_send.at[source, k], recv_sem=pair_recv.at[source, owner],
            device_id=at(me, lax.rem(pair + k, pairs) * 2 + core), device_id_type=MESH,
        )

    def core_copy(source, owner, side):
        where = pl.ds(pl.multiple_of((owner * 2 + side) * part, 16), part)
        return pltpu.make_async_remote_copy(
            src_ref=out_ref.at[source, where], dst_ref=out_ref.at[source, where],
            send_sem=core_send.at[source, owner], recv_sem=core_recv.at[source, owner],
            device_id=at(me, twin), device_id_type=MESH,
        )

    def push(k, carry):
        row_copy(k, me).start()
        return carry

    lax.fori_loop(1, peers, push, 0)
    local = pltpu.make_async_copy(panel.at[mine], out_ref.at[me, mine], home)
    local.start()
    local.wait()

    def relay(source):
        for k in range(1, pairs):
            pair_copy(source, k, pair).start()
        core_copy(source, pair, core).start()

    def onward(source):
        for k in range(1, pairs):
            owner = lax.rem(pair + k, pairs)
            pair_copy(source, k, owner).wait_recv()
            core_copy(source, owner, core).start()

    relay(me)

    def step(k, carry):
        source = lax.rem(me + peers - k, peers)
        row_copy(k, source).wait_recv()
        relay(source)
        onward(lax.rem(source + 1, peers))
        return carry

    lax.fori_loop(1, peers, step, 0)
    onward(lax.rem(me + 1, peers))

    def finish(source, carry):
        for owner in range(pairs):
            core_copy(source, owner, 1 - core).wait_recv()
            core_copy(source, owner, core).wait_send()
        for k in range(1, pairs):
            pair_copy(source, k, pair).wait_send()
        return carry

    lax.fori_loop(0, peers, finish, 0)

    def sent(k, carry):
        row_copy(k, me).wait_send()
        return carry

    lax.fori_loop(1, peers, sent, 0)

    @pl.when(col == 0)
    def _():
        def leads(k, carry):
            to = lax.rem(me + k, peers)
            for copy in lead_copy(to, to, me):
                copy.wait_send()
            return carry

        lax.fori_loop(1, peers, leads, 0)
        for index in range(1, cols):
            part_copy(index).wait_send()


def gather_panel(leads, targets, own):
    peers, cols = lax.axis_size("rows"), lax.axis_size("cols")
    pairs = cols // 2
    vmem = pl.BlockSpec(memory_space=pltpu.VMEM)
    dma = pltpu.SemaphoreType.DMA
    return pl.pallas_call(
        functools.partial(panel_kernel, peers, cols),
        out_shape=jax.ShapeDtypeStruct((peers,) + own.shape, jnp.bfloat16),
        in_specs=[vmem] * 3,
        out_specs=pl.BlockSpec(memory_space=pl.ANY),
        scratch_shapes=[
            pltpu.VMEM(leads.shape, leads.dtype),
            pltpu.VMEM(targets.shape, targets.dtype),
            pltpu.VMEM(own.shape, jnp.float32),
            pltpu.VMEM(own.shape, jnp.bfloat16),
            dma((peers,)), dma((peers,)), dma((peers,)), dma((peers,)),
            dma((cols,)), dma((cols,)),
            dma((peers,)), dma((peers,)),
            dma((peers, pairs)), dma((peers, pairs)),
            dma((peers, pairs)), dma((peers, pairs)),
            dma,
        ],
        compiler_params=pltpu.CompilerParams(
            collective_id=0, has_side_effects=True, vmem_limit_bytes=40 << 20
        ),
        cost_estimate=pl.CostEstimate(flops=1 << 30, bytes_accessed=8 << 20, transcendentals=0),
    )(leads, targets, own)


def on_device(front_rows, heights, child_rows, child_dest, child_slot, parent_ids):
    fronts, height_cap, width = front_rows.shape
    peers = lax.axis_size("rows")
    count = child_rows.shape[0]
    capacity = -(-max(2, 2 * count // peers) // NB) * NB
    slots = peers * capacity
    local_rows = fronts * height_cap
    destination = child_dest[:, 0]
    child_front = jnp.repeat(parent_ids, count // parent_ids.shape[0])
    hits = (destination[:, None] == jnp.arange(peers, dtype=jnp.int32)[None, :]).astype(jnp.bfloat16)
    earlier = (jnp.arange(count)[:, None] > jnp.arange(count)[None, :]).astype(jnp.bfloat16)
    before = jnp.dot(earlier, hits, preferred_element_type=jnp.float32)
    position = jnp.sum(before * hits.astype(jnp.float32), axis=1).astype(jnp.int32)
    send_index = destination * capacity + position
    packing = (jnp.arange(slots, dtype=jnp.int32)[:, None] == send_index[None, :]).astype(jnp.bfloat16)
    send_lead = jnp.dot(packing, child_rows[:, :NB], preferred_element_type=jnp.float32).astype(jnp.bfloat16)
    tags = jnp.stack([child_front, child_slot], axis=0).astype(jnp.bfloat16)
    send_tags = lax.dot_general(
        tags, packing, (((1,), (1,)), ((), ())), preferred_element_type=jnp.float32
    )
    targets = (send_tags[0] * height_cap + send_tags[1]).reshape(peers, capacity // NB, NB)
    targets = jnp.pad(targets, ((0, 0), (0, -(capacity // NB) % 8), (0, 0)))
    live_mask = jnp.arange(height_cap, dtype=jnp.int32)[None, :] < heights[0][:, None]
    own = jnp.where(live_mask[:, :, None], front_rows, jnp.zeros_like(front_rows))
    gathered = gather_panel(
        send_lead.reshape(peers, capacity, NB), targets, own[:, :, :NB].reshape(local_rows, NB)
    )
    panel_own = lax.dynamic_index_in_dim(gathered, lax.axis_index("rows"), 0, keepdims=False)
    panel_all = gathered.reshape(peers * local_rows, NB)
    by_front = panel_all.reshape(peers, fronts, height_cap, NB)
    gram = jnp.einsum("pfhk,pfhj->fkj", by_front, by_front, preferred_element_type=jnp.float32)
    key = destination * local_rows + child_front * height_cap + child_slot
    choosing = (key[:, None] == jnp.arange(peers * local_rows, dtype=jnp.int32)[None, :]).astype(jnp.bfloat16)
    selected = jnp.dot(choosing, panel_all, preferred_element_type=jnp.float32).astype(jnp.bfloat16)
    which = (jnp.arange(fronts, dtype=jnp.int32)[:, None] == child_front[None, :]).astype(jnp.bfloat16)
    picked = which[:, :, None] * selected[None, :, :]
    local = jnp.einsum("fsk,sc->fkc", picked, child_rows, preferred_element_type=jnp.float32)
    local = local + jnp.einsum(
        "fhk,fhc->fkc", panel_own.reshape(fronts, height_cap, NB), own, preferred_element_type=jnp.float32
    )
    norm = jnp.sqrt(jnp.sum(jnp.where(jnp.eye(NB, dtype=bool)[None], gram, 0.0), axis=1))
    reach = LARGEST * math.sqrt(height_cap + count) * math.sqrt(2 * count // peers + 2)
    scale = norm * (reach / 60000.0)
    local = local * (1.0 / scale)[:, :, None]
    parts = jnp.transpose(local.reshape(fronts, NB, peers, width // peers), (2, 0, 1, 3)).astype(jnp.float16)
    parts = lax.all_to_all(parts, "rows", split_axis=0, concat_axis=0, tiled=True)
    columns = jnp.sum(parts.astype(jnp.float32), axis=0) * scale[:, :, None]
    inverse = factor(gram)
    return jnp.einsum(
        "fij,fjc->fic", inverse, columns, precision=lax.Precision.HIGHEST, preferred_element_type=jnp.float32
    )


def solution(mesh):
    placed = (
        P(None, "rows", "cols"),
        P("rows", None),
        P("rows", "cols"),
        P("rows", None),
        P("rows"),
        P("rows"),
    )
    return jax.shard_map(
        on_device,
        mesh=mesh,
        in_specs=placed,
        out_specs=P(None, None, ("cols", "rows")),
        check_vma=False,
    )
```
